32 devices in a mesh: grp: 4 (over z), sp: 8 (over y, x, core).
Axes of the slice: x: 2, y: 2, z: 4, core: 2. Of those that a mesh axis runs over, the one named last changes fastest.
Arguments:
- tokens: bfloat16 [4096, 2880], P(('grp', 'sp')), may hold values from -6 to 6
- d_output: bfloat16 [4096, 2880], P(('grp', 'sp')), may hold values from -6 to 6
- expert_ids: int32 [4096, 2], P(('grp', 'sp')), may hold values from 0 to 63, all different within a row; in each aligned block of 128 rows (0 to 127, 128 to 255, ...) at most 8 rows name the same one
- route_weight: float32 [4096, 2], P(('grp', 'sp')), may hold values from 0.2 to 1
- gate_codes: bfloat16 [128, 2880, 720], P(('grp', 'sp')), may hold values from -1 to 1, as said below
- up_codes: bfloat16 [128, 2880, 720], P(('grp', 'sp')), may hold values from -1 to 1, as said below
- down_codes: bfloat16 [128, 720, 2880], P(('grp', 'sp')), may hold values from -1 to 1, as said below
- code_scales: float32 [64, 3], replicated, may hold values from 0.015 to 0.045
Outputs:
- output: bfloat16 [4096, 2880], P(('grp', 'sp'))
- d_tokens: bfloat16 [4096, 2880], P(('grp', 'sp'))
- d_route: float32 [4096, 2], P(('grp', 'sp'))
The draws below stay inside these ranges and needn't reach their ends.
Inputs may be any that keep to these rules, and one draw needn't show every extreme that they name: `expert_ids`: among the 128 x 2 entries of one device's tokens no expert appears more than 8 times, and some expert appears exactly 8 times; a token names 2 different experts. `gate_codes`: every entry is -1, 0 or 1. `up_codes`: every entry is -1, 0 or 1. `down_codes`: every entry is -1, 0 or 1.
All inputs are finite; a program needn't handle non-finite values.
Results may differ from the reference program's by a relative error of at most 0.0065.
Values may be sent and summed in bfloat16 or wider, within the bound.
No kernel may reach another device: no remote copies, remote signals or barrier semaphores. Data moves between devices by JAX's collectives and lax.ppermute only.
A program may use at most 192 MiB of HBM per device.

```python
import math
import jax
import jax.numpy as jnp
import numpy as np
from jax import lax

D = 2880
EXPERTS = 64
TOP = 2
TOK_DEV = 128
HH = 720
SHARDS = 128
CAP = 8
ROWS = 256
TOKENS = 4096


def ternary_draw(key, salt_value, shape):
    drawn_codes = jax.random.randint(jax.random.fold_in(key, salt_value), shape, -1, 2)
    return drawn_codes.astype(jnp.float32).astype(jnp.bfloat16)


def draw_gate_codes(key, part):
    return ternary_draw(key, 11, (SHARDS, D, HH))


def draw_up_codes(key, part):
    return ternary_draw(key, 23, (SHARDS, D, HH))


def draw_down_codes(key, part):
    return ternary_draw(key, 37, (SHARDS, HH, D))


def steps_of(own_key, dims, shards, smallest, largest):
    factor_of, own = 1.0, jax.random.fold_in(own_key, 6)
    for dim, shards_of in shards:
        steps = jnp.exp(jax.random.uniform(jax.random.fold_in(own, dim), (shards_of,), jnp.float32, smallest / len(shards), largest / len(shards)))
        factor_of = factor_of * jnp.repeat(steps, dims[dim] // shards_of).reshape([-1 if axis == dim else 1 for axis in range(len(dims))])
    return factor_of


def shared_out(rng, own, number, rows, number_of, top, limit, slope):
    order = jax.random.permutation(rng, number_of)
    packed, usual = load_shares(number_of, rows * top, limit, slope, True), load_shares(number_of, rows * top, limit, slope, False)
    places = jnp.arange(number_of)

    def named(tallies, offset_by):
        used = int((tallies > 0).sum())
        fixed = max(1, used // 4)
        passed = fixed + (places - fixed + offset_by * (used - fixed)) % max(1, number_of - fixed)
        return jnp.zeros((number_of,), jnp.int32).at[order[jnp.where(places < fixed, places, passed)]].set(jnp.asarray(tallies, jnp.int32))

    tallies = jnp.where(number % 4 == 0, named(packed, number // 4), named(usual, number - number // 4 - 1))
    mixed = jax.random.permutation(jax.random.fold_in(own, 3), number_of)
    donor, receiver = mixed[0:number_of // 2 * 2:2], mixed[1:number_of // 2 * 2:2]
    margin = jnp.minimum(tallies[donor] - 1, limit - tallies[receiver]) // 2
    margin = jnp.where((donor == order[0]) | (receiver == order[0]) | (tallies[receiver] == 0), 0, jnp.maximum(margin, 0))
    passed = jax.random.randint(jax.random.fold_in(own, 4), (number_of // 2,), 0, 1 << 20) % (margin + 1)
    tallies = tallies.at[donor].add(-passed).at[receiver].add(passed)
    items = jnp.searchsorted(jnp.cumsum(tallies), jnp.arange(rows * top), side="right").astype(jnp.int32)
    grid = items.reshape(top, rows).T
    grid = grid[jax.random.permutation(jax.random.fold_in(own, 1), rows)]
    offset_by = jax.random.randint(jax.random.fold_in(own, 2), (rows, 1), 0, top)
    return jnp.take_along_axis(grid, (jnp.arange(top)[None, :] + offset_by) % top, axis=1)


def load_shares(count, total, reach, skew, full):
    portions = [(1 << 20) // math.isqrt(rank ** skew) + 1 for rank in range(1, count + 1)]
    largest = reach if full else min(reach, max(-(-total // count), total * portions[0] // sum(portions)))
    least = 1 if total - largest >= count - 1 else 0
    given, rest = [largest] + [least] * (count - 1), total - largest - least * (count - 1)
    while rest > 0:
        candidates = [i for i in range(1, count) if given[i] < largest] or [i for i in range(1, count) if given[i] < reach]
        mass, remaining = sum([portions[i] for i in candidates]), rest
        for i in candidates:
            extra = min(reach - given[i], max(1, remaining * portions[i] // mass), rest)
            given[i] = given[i] + extra
            rest = rest - extra
    return np.array(given)


def centred(rng, extent, deviation, limit, pieces=(), kind=jnp.bfloat16):
    level = steps_of(rng, extent, pieces, -0.22, 0.18) if pieces else 1.0
    drawn = jax.random.normal(rng, extent, jnp.float32) * deviation * level
    return jnp.minimum(jnp.maximum(drawn, -limit), limit).astype(kind)


def setup_inputs(seed: int = 0) -> dict:
    keys = jax.random.split(jax.random.key(seed), 9)
    tokens = centred(keys[0], (TOKENS, D), 1.0, 6.0, ((0, 32),))
    d_output = centred(keys[1], (TOKENS, D), 1.0, 6.0, ((0, 32),))
    expert_ids_keys = jax.random.split(jax.random.fold_in(keys[2], 1), TOKENS // TOK_DEV)
    expert_ids_turns = jax.random.permutation(jax.random.fold_in(keys[2], 3), TOKENS // TOK_DEV)
    expert_ids = jax.vmap(lambda own, number: shared_out(jax.random.fold_in(keys[2], 2), own, number, TOK_DEV, EXPERTS, TOP, CAP, 2))(expert_ids_keys, expert_ids_turns).reshape((TOKENS, TOP))
    route_weight = jnp.clip(0.2 + 0.8 * jax.random.uniform(keys[3], (TOKENS, TOP), jnp.float32) ** steps_of(keys[3], (TOKENS, TOP), ((0, 32),), -0.2, 0.2), 0.2, 1.0)
    gate_codes = draw_gate_codes(jax.random.fold_in(keys[8], 71), 0)
    up_codes = draw_up_codes(jax.random.fold_in(keys[8], 71), 0)
    down_codes = draw_down_codes(jax.random.fold_in(keys[8], 71), 0)
    code_scales = jnp.clip(jnp.exp(jax.random.uniform(keys[7], (EXPERTS, 3), jnp.float32, math.log(0.015), math.log(0.045))), 0.015, 0.045)
    return {"tokens": tokens, "d_output": d_output, "expert_ids": expert_ids, "route_weight": route_weight, "gate_codes": gate_codes, "up_codes": up_codes, "down_codes": down_codes, "code_scales": code_scales}


def slot_ranks(expert_ids):
    blocks = expert_ids.reshape(TOKENS // TOK_DEV, TOK_DEV * TOP)
    labels = jnp.arange(EXPERTS, dtype=jnp.int32)
    onehot = (blocks[:, :, None] == labels[None, None, :]).astype(jnp.int32)
    before = jnp.cumsum(onehot, axis=1) - onehot
    return jnp.sum(before * onehot, axis=2).reshape(TOKENS, TOP)


def expert_pass(rows_in, grad_in, gate_matrix, up_matrix, down_matrix, scales):
    gate_value = scales[0] * jnp.dot(rows_in, gate_matrix, preferred_element_type=jnp.float32)
    up_value = scales[1] * jnp.dot(rows_in, up_matrix, preferred_element_type=jnp.float32)
    sigmoid_gate = 1.0 / (1.0 + jnp.exp(-gate_value))
    silu_gate = gate_value * sigmoid_gate
    activation = (silu_gate * up_value).astype(jnp.bfloat16)
    expert_part = scales[2] * jnp.dot(activation, down_matrix, preferred_element_type=jnp.float32)
    grad_activation = scales[2] * jnp.dot(grad_in, down_matrix.T, preferred_element_type=jnp.float32)
    grad_gate = (grad_activation * up_value * sigmoid_gate * (1.0 + gate_value * (1.0 - sigmoid_gate))).astype(jnp.bfloat16)
    grad_up = (grad_activation * silu_gate).astype(jnp.bfloat16)
    grad_part = scales[0] * jnp.dot(grad_gate, gate_matrix.T, preferred_element_type=jnp.float32)
    grad_part = grad_part + scales[1] * jnp.dot(grad_up, up_matrix.T, preferred_element_type=jnp.float32)
    return expert_part, grad_part


def reference(tokens, d_output, expert_ids, route_weight, gate_codes, up_codes, down_codes, code_scales):
    slot_rank = slot_ranks(expert_ids)
    source = (jnp.arange(TOKENS, dtype=jnp.int32) // TOK_DEV)[:, None]
    target = (expert_ids * ROWS + source * CAP + slot_rank).reshape(-1).astype(jnp.int32)
    token_rows = jnp.repeat(tokens, TOP, axis=0)
    scaled = (route_weight[:, :, None] * d_output.astype(jnp.float32)[:, None, :]).astype(jnp.bfloat16)
    scaled = scaled.reshape(TOKENS * TOP, D)
    inputs = jnp.zeros((EXPERTS * ROWS, D), token_rows.dtype).at[target].set(token_rows).reshape(EXPERTS, ROWS, D)
    grad_rows = jnp.zeros((EXPERTS * ROWS, D), scaled.dtype).at[target].set(scaled).reshape(EXPERTS, ROWS, D)

    def per_expert(expert):
        rows_in = inputs[expert]
        grad_in = grad_rows[expert]
        scales = code_scales[expert]
        other = expert + EXPERTS
        lower_half = expert_pass(rows_in, grad_in, gate_codes[expert], up_codes[expert], down_codes[expert], scales)
        upper_half = expert_pass(rows_in, grad_in, gate_codes[other], up_codes[other], down_codes[other], scales)
        expert_out = (lower_half[0] + upper_half[0]).astype(jnp.bfloat16)
        expert_grad = (lower_half[1] + upper_half[1]).astype(jnp.bfloat16)
        return expert_out, expert_grad

    expert_outs, expert_grads = lax.map(per_expert, jnp.arange(EXPERTS, dtype=jnp.int32))
    picked = expert_outs.reshape(EXPERTS * ROWS, D)[target].astype(jnp.float32).reshape(TOKENS, TOP, D)
    picked_grad = expert_grads.reshape(EXPERTS * ROWS, D)[target].astype(jnp.float32).reshape(TOKENS, TOP, D)
    output = jnp.sum(route_weight[:, :, None] * picked, axis=1).astype(jnp.bfloat16)
    d_route = jnp.sum(d_output.astype(jnp.float32)[:, None, :] * picked, axis=2)
    d_tokens = jnp.sum(picked_grad, axis=1).astype(jnp.bfloat16)
    return (output, d_tokens, d_route)
```

```python
import functools

import jax
import jax.numpy as jnp
from jax import lax
from jax.experimental import pallas as pl
from jax.experimental.pallas import tpu as pltpu
from jax.sharding import PartitionSpec as P

AXES = ("grp", "sp")
CORE, COL, ROW = 1, 2, 4
VMEM_BYTES = 56 * 1024 * 1024
F32, BF16 = jnp.float32, jnp.bfloat16


def silu_parts(gate_value):
    sigmoid_gate = 1.0 / (1.0 + jnp.exp(-gate_value))
    return (sigmoid_gate, gate_value * sigmoid_gate)


def per_device(
    tokens, d_output, expert_ids, route_weight, gate_codes, up_codes, down_codes, code_scales
):
    tok_rows, width = tokens.shape
    top_count = expert_ids.shape[1]
    shards_here = gate_codes.shape[0]
    expert_count = code_scales.shape[0]
    group_count = lax.axis_size("grp")
    inner_count = lax.axis_size("sp")
    device_count = group_count * inner_count
    slot_count = 2 * tok_rows * top_count // expert_count
    flat_ids = expert_ids.reshape(-1)
    labels = jnp.arange(expert_count, dtype=jnp.int32)
    onehot = (flat_ids[:, None] == labels[None, :]).astype(jnp.int32)
    slot_rank = jnp.sum((jnp.cumsum(onehot, axis=0) - onehot) * onehot, axis=1)
    target = flat_ids * slot_count + slot_rank
    cells = jnp.arange(expert_count * slot_count, dtype=jnp.int32)
    placing = (target[:, None] == cells[None, :]).astype(jnp.bfloat16)
    token_rows = jnp.repeat(tokens, top_count, axis=0)
    grad_rows = jnp.repeat(d_output, top_count, axis=0).astype(jnp.float32)
    scaled = (route_weight.reshape(-1)[:, None] * grad_rows).astype(jnp.bfloat16)
    payload = jnp.concatenate([token_rows, scaled], axis=1)
    arranged = lax.dot_general(
        placing, payload, (((0,), (0,)), ((), ())), preferred_element_type=jnp.float32
    )
    arranged = arranged.astype(jnp.bfloat16).reshape(expert_count, slot_count, 2 * width)
    arranged = jnp.concatenate([arranged, arranged], axis=0)
    rows_out = arranged[:, :, :width]
    grads_out = arranged[:, :, width:]
    direct_shape = (device_count, shards_here, slot_count, width)
    rows_in, grads_in = (
        lax.all_to_all(rows_out.reshape(direct_shape), AXES, split_axis=0, concat_axis=0, tiled=True),
        lax.all_to_all(grads_out.reshape(direct_shape), AXES, split_axis=0, concat_axis=0, tiled=True),
    )
    device_index = lax.axis_index("grp") * inner_count + lax.axis_index("sp")
    first_shard = device_index * shards_here
    scales_here = lax.dynamic_slice_in_dim(code_scales, first_shard % expert_count, shards_here, 0)
    scale_gate = scales_here[:, 0][None, :, None, None]
    scale_up = scales_here[:, 1][None, :, None, None]
    scale_down = scales_here[:, 2][None, :, None, None]

    def product(spec, left, right):
        return jnp.einsum(spec, left, right, preferred_element_type=jnp.float32)

    gate_value = product("nicd,idh->nich", rows_in, gate_codes) * scale_gate
    up_value = product("nicd,idh->nich", rows_in, up_codes) * scale_up
    sigmoid_gate, silu_gate = silu_parts(gate_value)
    activation = (silu_gate * up_value).astype(jnp.bfloat16)
    expert_part = product("nich,ihd->nicd", activation, down_codes) * scale_down
    grad_activation = product("nicd,ihd->nich", grads_in, down_codes) * scale_down
    grad_gate = (
        grad_activation * up_value * sigmoid_gate * (1.0 + gate_value * (1.0 - sigmoid_gate))
    ).astype(jnp.bfloat16)
    grad_up = (grad_activation * silu_gate).astype(jnp.bfloat16)
    grad_part = product("nich,idh->nicd", grad_gate, gate_codes) * scale_gate
    grad_part = grad_part + product("nich,idh->nicd", grad_up, up_codes) * scale_up
    returned_part, returned_grad = (
        lax.all_to_all(expert_part.astype(BF16), AXES, split_axis=0, concat_axis=0, tiled=True),
        lax.all_to_all(grad_part.astype(BF16), AXES, split_axis=0, concat_axis=0, tiled=True),
    )
    returned_part = returned_part.reshape(2 * expert_count, slot_count, width).astype(F32)
    returned_grad = returned_grad.reshape(2 * expert_count, slot_count, width).astype(F32)
    expert_out = (returned_part[:expert_count] + returned_part[expert_count:]).astype(jnp.bfloat16)
    expert_grad = (returned_grad[:expert_count] + returned_grad[expert_count:]).astype(jnp.bfloat16)
    gathered = jnp.concatenate(
        [expert_out.reshape(-1, width), expert_grad.reshape(-1, width)], axis=1
    )
    picked = jnp.dot(placing, gathered, preferred_element_type=jnp.float32)
    picked_out = picked[:, :width].reshape(tok_rows, top_count, width)
    picked_grad = picked[:, width:].reshape(tok_rows, top_count, width)
    output = jnp.sum(route_weight[:, :, None] * picked_out, axis=1).astype(jnp.bfloat16)
    d_route = jnp.sum(d_output.astype(jnp.float32)[:, None, :] * picked_out, axis=2)
    d_tokens = jnp.sum(picked_grad, axis=1).astype(jnp.bfloat16)
    return (output, d_tokens, d_route)


def hub_onehots(pos_ref, info, slots, experts):
    plane, here = pos_ref[0], pos_ref[1]
    far = jnp.where(here % 2 == 0, ROW, COL)
    tokens = info.shape[1]
    rows = 4 * experts * 2 * slots
    row = lax.broadcasted_iota(jnp.int32, (rows, 1), 0)
    message = row // (2 * slots * experts)
    expert = (row // (2 * slots)) % experts
    side = (row // slots) % 2
    base = (plane % 2) * 8
    device = jnp.where(
        message == 0,
        base + here,
        jnp.where(
            message == 1,
            base + (here ^ CORE),
            jnp.where(message == 2, base + (here ^ far), base + (here ^ far ^ CORE)),
        ),
    )
    cell = ((side * 16 + device) * experts + expert) * slots + row % slots
    column = lax.broadcasted_iota(jnp.int32, (1, tokens), 1)
    partner = (column // (tokens // 2)) * 16 * experts
    first = (partner + info[0:1].astype(jnp.int32)) * slots + info[2:3].astype(jnp.int32)
    second = (partner + info[1:2].astype(jnp.int32)) * slots + info[3:4].astype(jnp.int32)
    weight_first = info[4:5] + info[6:7] + info[8:9]
    weight_second = info[5:6] + info[7:8] + info[9:10]
    return first == cell, second == cell, weight_first, weight_second


def routing(own_ref, other_ref):
    return jnp.concatenate([own_ref[...], other_ref[...]], axis=1).astype(F32)


def dot_nt(left, right):
    return lax.dot_general(left, right, (((1,), (1,)), ((), ())), preferred_element_type=F32)


def dot_tn(left, right):
    return lax.dot_general(left, right, (((0,), (0,)), ((), ())), preferred_element_type=F32)


def pack_kernel(
    slots, experts, scaled, pos_ref, own_info, other_info, own_ref, other_ref, kept_ref, core_ref, far_ref
):
    first, second, weight_first, weight_second = hub_onehots(
        pos_ref, routing(own_info, other_info), slots, experts
    )
    chosen = (first | second).astype(F32).astype(BF16)
    half = own_ref.shape[1]
    rows = dot_nt(chosen[:, :half], own_ref[...]) + dot_nt(chosen[:, half:], other_ref[...])
    if scaled:
        weight = jnp.where(first, weight_first, 0.0) + jnp.where(second, weight_second, 0.0)
        rows = rows * jnp.sum(weight, axis=1, keepdims=True)
    rows = rows.astype(BF16)
    size = rows.shape[0] // 4
    kept_ref[...] = rows[:size]
    core_ref[...] = rows[size : 2 * size]
    far_ref[0] = rows[2 * size : 3 * size]
    far_ref[1] = rows[3 * size :]


def combine_kernel(
    slots, experts, pos_ref, own_info, other_info, kept_ref, core_ref, far_ref, own_ref, other_ref
):
    first, second, _, _ = hub_onehots(pos_ref, routing(own_info, other_info), slots, experts)
    chosen = (first | second).astype(F32).astype(BF16)
    rows = jnp.concatenate([kept_ref[...], core_ref[0], far_ref[0], far_ref[1]], axis=0)
    half = own_ref.shape[1]
    sums = dot_tn(rows, chosen)
    own_ref[...] = sums[:, :half]
    other_ref[...] = sums[:, half:].astype(BF16)


def combine_out_kernel(
    slots,
    experts,
    pos_ref,
    own_info,
    other_info,
    kept_ref,
    core_ref,
    far_ref,
    d_own_ref,
    d_other_ref,
    own_ref,
    other_ref,
    route_ref,
):
    first, second, weight_first, weight_second = hub_onehots(
        pos_ref, routing(own_info, other_info), slots, experts
    )
    weight = jnp.where(first, weight_first, 0.0) + jnp.where(second, weight_second, 0.0)
    high = weight.astype(BF16)
    low = (weight - high.astype(F32)).astype(BF16)
    rows = jnp.concatenate([kept_ref[...], core_ref[0], far_ref[0], far_ref[1]], axis=0)
    half = own_ref.shape[1]
    sums = dot_tn(rows, high) + dot_tn(rows, low)
    own_ref[...] = sums[:, :half]
    other_ref[...] = sums[:, half:].astype(BF16)
    for side, d_ref in enumerate((d_own_ref, d_other_ref)):
        span = slice(side * half, (side + 1) * half)
        dots = jnp.dot(rows, d_ref[...], preferred_element_type=F32)
        for choice, mask in enumerate((first, second)):
            route_ref[side, choice : choice + 1, :] = jnp.sum(
                jnp.where(mask[:, span], dots, 0.0), axis=0, keepdims=True
            )


def rows_of(refs):
    parts = []
    for kept_ref, far_ref, core_ref in zip(refs[0::3], refs[1::3], refs[2::3]):
        parts += [kept_ref[...], far_ref[0], core_ref[0], core_ref[1]]
    return jnp.concatenate(parts, axis=0)


def put_rows(refs, value):
    size = refs[0].shape[0]
    for plane in range(len(refs) // 3):
        kept_ref, far_ref, core_ref = refs[3 * plane : 3 * plane + 3]
        part = [value[(4 * plane + n) * size : (4 * plane + n + 1) * size] for n in range(4)]
        kept_ref[...], far_ref[...], core_ref[0], core_ref[1] = part


def experts_kernel(experts, planes, pos_ref, scales_ref, *refs):
    count = 3 * planes
    x_refs, d_refs, refs = refs[:count], refs[count : 2 * count], refs[2 * count :]
    (gate_ref, up_ref, down_ref), out_refs, grad_refs = refs[:3], refs[3 : 3 + count], refs[3 + count :]
    expert = ((pos_ref[0] % 2) * 8 + pos_ref[1]) * experts + pl.program_id(0)
    scale_gate, scale_up, scale_down = [scales_ref[expert, n] for n in range(3)]
    x = rows_of(x_refs)
    gate_value = dot_nt(x, gate_ref[0]) * scale_gate
    up_value = dot_nt(x, up_ref[0]) * scale_up
    grad_activation = dot_nt(rows_of(d_refs), down_ref[0]) * scale_down
    sigmoid_gate, silu_gate = silu_parts(gate_value)
    activation = (silu_gate * up_value).astype(BF16)
    grad_gate = grad_activation * up_value * sigmoid_gate * (1.0 + gate_value * (1.0 - sigmoid_gate))
    grad_gate = grad_gate.astype(BF16)
    grad_up = (grad_activation * silu_gate).astype(BF16)
    part = jnp.dot(activation, down_ref[0], preferred_element_type=F32) * scale_down
    put_rows(out_refs, part.astype(BF16))
    part = jnp.dot(grad_gate, gate_ref[0], preferred_element_type=F32) * scale_gate
    part = part + jnp.dot(grad_up, up_ref[0], preferred_element_type=F32) * scale_up
    put_rows(grad_refs, part.astype(BF16))


SMEM_SPEC = pl.BlockSpec(memory_space=pltpu.SMEM)
PARAMS = pltpu.CompilerParams(vmem_limit_bytes=VMEM_BYTES)


def whole(*shape):
    return pl.BlockSpec(shape, lambda i: (0,) * len(shape))


def after(value, *others):
    return lax.optimization_barrier((value, *others))[0]


def with_core(value):
    return lax.ppermute(value, AXES, [(n, n ^ CORE) for n in range(32)])


def with_near(value):
    return lax.ppermute(value, AXES, [(n, n ^ (ROW if n & CORE else COL)) for n in range(32)])


def with_far(value):
    return lax.ppermute(value, AXES, [(n, n ^ (COL if n & CORE else ROW)) for n in range(32)])


def to_next_plane(value, by):
    return lax.ppermute(value, AXES, [(n, (n + 8 * by) % 32) for n in range(32)])


def per_device_planes(
    tokens, d_output, expert_ids, route_weight, gate_codes, up_codes, down_codes, code_scales
):
    tokens, d_output, ids = tokens.T, d_output.T, expert_ids.T
    gate_codes, up_codes = jnp.swapaxes(gate_codes, 1, 2), jnp.swapaxes(up_codes, 1, 2)
    width, tok_rows = tokens.shape
    experts, hidden = gate_codes.shape[:2]
    expert_count = code_scales.shape[0]
    slots = 2 * tok_rows * ids.shape[0] // expert_count
    message = experts * 2 * slots
    pos = jnp.stack([lax.axis_index("grp"), lax.axis_index("sp")]).astype(jnp.int32)

    earlier = jnp.arange(tok_rows)[:, None] < jnp.arange(tok_rows)[None, :]
    same = (ids[:, None, :, None] == ids[None, :, None, :]) & earlier
    rank = jnp.sum(same.astype(jnp.int32), axis=(0, 2))
    weight = route_weight.T
    high = lax.reduce_precision(weight, 8, 7)
    middle = lax.reduce_precision(weight - high, 8, 7)
    low = weight - high - middle
    info = [ids.astype(F32), rank.astype(F32), high, middle, low]
    info = jnp.concatenate(info + [jnp.zeros((6, tok_rows), F32)], axis=0).astype(BF16)
    tokens = jnp.concatenate([tokens, info], axis=0)
    info_rows = info.shape[0]

    one_type = jax.ShapeDtypeStruct((message, width), BF16)
    two_type = jax.ShapeDtypeStruct((2, message, width), BF16)
    info_spec = pl.BlockSpec((info_rows, tok_rows), lambda i: (width // info_rows, 0))
    block_spec = whole(width, tok_rows)
    one_spec, two_spec = whole(message, width), whole(2, message, width)
    first_spec = pl.BlockSpec((1, message, width), lambda i: (0, 0, 0))
    small_cost = pl.CostEstimate(
        flops=4 * message * 4 * tok_rows * width, bytes_accessed=12 * message * width, transcendentals=0
    )

    def spread(rows, infos, scaled):
        arrived, raw = [], []
        for step in range(4):
            other = with_near(rows)
            raw.append((rows, other))
            kept, core, far = pl.pallas_call(
                functools.partial(pack_kernel, slots, experts, scaled),
                out_shape=[one_type, one_type, two_type],
                grid=(1,),
                in_specs=[SMEM_SPEC] + [info_spec] * 2 + [block_spec] * 2,
                out_specs=[one_spec, one_spec, two_spec],
                compiler_params=PARAMS,
                cost_estimate=small_cost,
                name="pack_gradients" if scaled else "pack_tokens",
            )(pos, *(infos or raw)[step], rows, other)
            far = with_far(far)
            core = with_core(jnp.stack([core, far[1]]))
            arrived += [kept, far, core]
            if step < 3:
                rows = to_next_plane(rows, 1)
        return arrived, raw

    token_rows, infos = spread(tokens, None, False)
    grad_rows, raw_grads = spread(d_output, infos, True)

    expert_rows = 2 * slots
    kept_in = pl.BlockSpec((expert_rows, width), lambda i: (i, 0))
    far_in = pl.BlockSpec((1, expert_rows, width), lambda i: (0, i, 0))
    core_in = pl.BlockSpec((2, expert_rows, width), lambda i: (0, i, 0))
    code_spec = pl.BlockSpec((1, hidden, width), lambda i: (i, 0, 0))

    def run_experts(steps):
        planes = len(steps)
        span = slice(3 * steps[0], 3 * steps[0] + 3 * planes)
        row_count = planes * 4 * expert_rows
        done = pl.pallas_call(
            functools.partial(experts_kernel, experts, planes),
            out_shape=[one_type, one_type, two_type] * (2 * planes),
            grid=(experts,),
            in_specs=[SMEM_SPEC] * 2
            + [kept_in, far_in, core_in] * (2 * planes)
            + [code_spec] * 3,
            out_specs=[kept_in, kept_in, core_in] * (2 * planes),
            compiler_params=PARAMS,
            cost_estimate=pl.CostEstimate(
                flops=experts * row_count * width * hidden * 12,
                bytes_accessed=experts * width * hidden * 6,
                transcendentals=experts * row_count * hidden,
            ),
            name="experts",
        )(pos, code_scales, *token_rows[span], *grad_rows[span], gate_codes, up_codes, down_codes)
        return done[: 3 * planes], done[3 * planes :]

    parts, grads = run_experts((0, 1, 2, 3))

    own_type = jax.ShapeDtypeStruct((width, tok_rows), F32)
    other_type = jax.ShapeDtypeStruct((width, tok_rows), BF16)
    route_type = jax.ShapeDtypeStruct((2, 2, tok_rows), F32)

    def gather(rows, outputs):
        total, routes, last = None, [None] * 4, []
        for step in (3, 2, 1, 0):
            kept, far, core = rows[3 * step : 3 * step + 3]
            core = with_core(core)
            far = with_far(after(jnp.stack([far, core[1]]), *last))
            own, other, *route = pl.pallas_call(
                functools.partial(combine_out_kernel if outputs else combine_kernel, slots, experts),
                out_shape=[own_type, other_type] + [route_type] * outputs,
                grid=(1,),
                in_specs=[SMEM_SPEC]
                + [info_spec] * 2
                + [one_spec, first_spec, two_spec]
                + [block_spec] * (2 * outputs),
                out_specs=[block_spec] * 2 + [whole(2, 2, tok_rows)] * outputs,
                compiler_params=PARAMS,
                cost_estimate=small_cost,
                name="sum_outputs" if outputs else "sum_gradients",
            )(pos, *infos[step], kept, core, far, *(raw_grads[step] if outputs else ()))
            routes[step] = route
            other = with_near(other)
            last = [other]
            value = own + other.astype(F32)
            if total is not None:
                value = value + to_next_plane(total, -1).astype(F32)
            total = value.astype(BF16)
        return total, routes

    output, routes = gather(parts, 1)
    route = jnp.stack([r[0][0] for r in routes]) + with_near(jnp.stack([r[0][1] for r in routes]))
    d_route = route[0]
    for step in (1, 2, 3):
        d_route = d_route + to_next_plane(route[step], -step)
    d_tokens, _ = gather(grads, 0)
    return (output.T, d_tokens.T, d_route.T)


def solution(mesh):
    planes = mesh.shape["grp"] == 4 and mesh.shape["sp"] == 8
    spec = P(AXES, None)
    codes = P(AXES, None, None)
    return jax.shard_map(
        per_device_planes if planes else per_device,
        mesh=mesh,
        in_specs=(spec, spec, spec, spec, codes, codes, codes, P()),
        out_specs=(spec, spec, spec),
        check_vma=False,
    )
```

```python
import functools

import jax
import jax.numpy as jnp
from jax import lax
from jax.experimental import pallas as pl
from jax.experimental.pallas import tpu as pltpu
from jax.sharding import PartitionSpec as P

AXES = ("grp", "sp")
CORE, COL, ROW = 1, 2, 4
VMEM_BYTES = 56 * 1024 * 1024
F32, BF16 = jnp.float32, jnp.bfloat16


def silu_parts(gate_value):
    sigmoid_gate = 1.0 / (1.0 + jnp.exp(-gate_value))
    return (sigmoid_gate, gate_value * sigmoid_gate)


def per_device(
    tokens, d_output, expert_ids, route_weight, gate_codes, up_codes, down_codes, code_scales
):
    tok_rows, width = tokens.shape
    top_count = expert_ids.shape[1]
    shards_here = gate_codes.shape[0]
    expert_count = code_scales.shape[0]
    group_count = lax.axis_size("grp")
    inner_count = lax.axis_size("sp")
    device_count = group_count * inner_count
    slot_count = 2 * tok_rows * top_count // expert_count
    flat_ids = expert_ids.reshape(-1)
    labels = jnp.arange(expert_count, dtype=jnp.int32)
    onehot = (flat_ids[:, None] == labels[None, :]).astype(jnp.int32)
    slot_rank = jnp.sum((jnp.cumsum(onehot, axis=0) - onehot) * onehot, axis=1)
    target = flat_ids * slot_count + slot_rank
    cells = jnp.arange(expert_count * slot_count, dtype=jnp.int32)
    placing = (target[:, None] == cells[None, :]).astype(jnp.bfloat16)
    token_rows = jnp.repeat(tokens, top_count, axis=0)
    grad_rows = jnp.repeat(d_output, top_count, axis=0).astype(jnp.float32)
    scaled = (route_weight.reshape(-1)[:, None] * grad_rows).astype(jnp.bfloat16)
    payload = jnp.concatenate([token_rows, scaled], axis=1)
    arranged = lax.dot_general(
        placing, payload, (((0,), (0,)), ((), ())), preferred_element_type=jnp.float32
    )
    arranged = arranged.astype(jnp.bfloat16).reshape(expert_count, slot_count, 2 * width)
    arranged = jnp.concatenate([arranged, arranged], axis=0)
    rows_out = arranged[:, :, :width]
    grads_out = arranged[:, :, width:]
    direct_shape = (device_count, shards_here, slot_count, width)
    rows_in, grads_in = (
        lax.all_to_all(rows_out.reshape(direct_shape), AXES, split_axis=0, concat_axis=0, tiled=True),
        lax.all_to_all(grads_out.reshape(direct_shape), AXES, split_axis=0, concat_axis=0, tiled=True),
    )
    device_index = lax.axis_index("grp") * inner_count + lax.axis_index("sp")
    first_shard = device_index * shards_here
    scales_here = lax.dynamic_slice_in_dim(code_scales, first_shard % expert_count, shards_here, 0)
    scale_gate = scales_here[:, 0][None, :, None, None]
    scale_up = scales_here[:, 1][None, :, None, None]
    scale_down = scales_here[:, 2][None, :, None, None]

    def product(spec, left, right):
        return jnp.einsum(spec, left, right, preferred_element_type=jnp.float32)

    gate_value = product("nicd,idh->nich", rows_in, gate_codes) * scale_gate
    up_value = product("nicd,idh->nich", rows_in, up_codes) * scale_up
    sigmoid_gate, silu_gate = silu_parts(gate_value)
    activation = (silu_gate * up_value).astype(jnp.bfloat16)
    expert_part = product("nich,ihd->nicd", activation, down_codes) * scale_down
    grad_activation = product("nicd,ihd->nich", grads_in, down_codes) * scale_down
    grad_gate = (
        grad_activation * up_value * sigmoid_gate * (1.0 + gate_value * (1.0 - sigmoid_gate))
    ).astype(jnp.bfloat16)
    grad_up = (grad_activation * silu_gate).astype(jnp.bfloat16)
    grad_part = product("nich,idh->nicd", grad_gate, gate_codes) * scale_gate
    grad_part = grad_part + product("nich,idh->nicd", grad_up, up_codes) * scale_up
    returned_part, returned_grad = (
        lax.all_to_all(expert_part.astype(BF16), AXES, split_axis=0, concat_axis=0, tiled=True),
        lax.all_to_all(grad_part.astype(BF16), AXES, split_axis=0, concat_axis=0, tiled=True),
    )
    returned_part = returned_part.reshape(2 * expert_count, slot_count, width).astype(F32)
    returned_grad = returned_grad.reshape(2 * expert_count, slot_count, width).astype(F32)
    expert_out = (returned_part[:expert_count] + returned_part[expert_count:]).astype(jnp.bfloat16)
    expert_grad = (returned_grad[:expert_count] + returned_grad[expert_count:]).astype(jnp.bfloat16)
    gathered = jnp.concatenate(
        [expert_out.reshape(-1, width), expert_grad.reshape(-1, width)], axis=1
    )
    picked = jnp.dot(placing, gathered, preferred_element_type=jnp.float32)
    picked_out = picked[:, :width].reshape(tok_rows, top_count, width)
    picked_grad = picked[:, width:].reshape(tok_rows, top_count, width)
    output = jnp.sum(route_weight[:, :, None] * picked_out, axis=1).astype(jnp.bfloat16)
    d_route = jnp.sum(d_output.astype(jnp.float32)[:, None, :] * picked_out, axis=2)
    d_tokens = jnp.sum(picked_grad, axis=1).astype(jnp.bfloat16)
    return (output, d_tokens, d_route)


def hub_onehots(pos_ref, info, slots, experts):
    plane, here = pos_ref[0], pos_ref[1]
    far = jnp.where(here % 2 == 0, ROW, COL)
    tokens = info.shape[1]
    rows = 4 * experts * 2 * slots
    row = lax.broadcasted_iota(jnp.int32, (rows, 1), 0)
    message = row // (2 * slots * experts)
    expert = (row // (2 * slots)) % experts
    side = (row // slots) % 2
    base = (plane % 2) * 8
    device = jnp.where(
        message == 0,
        base + here,
        jnp.where(
            message == 1,
            base + (here ^ CORE),
            jnp.where(message == 2, base + (here ^ far), base + (here ^ far ^ CORE)),
        ),
    )
    cell = ((side * 16 + device) * experts + expert) * slots + row % slots
    column = lax.broadcasted_iota(jnp.int32, (1, tokens), 1)
    partner = (column // (tokens // 2)) * 16 * experts
    first = (partner + info[0:1].astype(jnp.int32)) * slots + info[2:3].astype(jnp.int32)
    second = (partner + info[1:2].astype(jnp.int32)) * slots + info[3:4].astype(jnp.int32)
    weight_first = info[4:5] + info[6:7] + info[8:9]
    weight_second = info[5:6] + info[7:8] + info[9:10]
    return first == cell, second == cell, weight_first, weight_second


def routing(own_ref, other_ref):
    return jnp.concatenate([own_ref[...], other_ref[...]], axis=1).astype(F32)


def dot_nt(left, right):
    return lax.dot_general(left, right, (((1,), (1,)), ((), ())), preferred_element_type=F32)


def dot_tn(left, right):
    return lax.dot_general(left, right, (((0,), (0,)), ((), ())), preferred_element_type=F32)


def pack_kernel(
    slots, experts, scaled, pos_ref, own_info, other_info, own_ref, other_ref, kept_ref, core_ref, far_ref
):
    first, second, weight_first, weight_second = hub_onehots(
        pos_ref, routing(own_info, other_info), slots, experts
    )
    chosen = (first | second).astype(F32).astype(BF16)
    half = own_ref.shape[1]
    rows = dot_nt(chosen[:, :half], own_ref[...]) + dot_nt(chosen[:, half:], other_ref[...])
    if scaled:
        weight = jnp.where(first, weight_first, 0.0) + jnp.where(second, weight_second, 0.0)
        rows = rows * jnp.sum(weight, axis=1, keepdims=True)
    rows = rows.astype(BF16)
    size = rows.shape[0] // 4
    kept_ref[...] = rows[:size]
    core_ref[...] = rows[size : 2 * size]
    far_ref[0] = rows[2 * size : 3 * size]
    far_ref[1] = rows[3 * size :]


def combine_kernel(
    slots, experts, pos_ref, own_info, other_info, kept_ref, core_ref, far_ref, own_ref, other_ref
):
    first, second, _, _ = hub_onehots(pos_ref, routing(own_info, other_info), slots, experts)
    chosen = (first | second).astype(F32).astype(BF16)
    rows = jnp.concatenate([kept_ref[...], core_ref[0], far_ref[0], far_ref[1]], axis=0)
    half = own_ref.shape[1]
    sums = dot_tn(rows, chosen)
    own_ref[...] = sums[:, :half]
    other_ref[...] = sums[:, half:].astype(BF16)


def combine_out_kernel(
    slots,
    experts,
    pos_ref,
    own_info,
    other_info,
    kept_ref,
    core_ref,
    far_ref,
    d_own_ref,
    d_other_ref,
    own_ref,
    other_ref,
    route_ref,
):
    first, second, weight_first, weight_second = hub_onehots(
        pos_ref, routing(own_info, other_info), slots, experts
    )
    weight = jnp.where(first, weight_first, 0.0) + jnp.where(second, weight_second, 0.0)
    high = weight.astype(BF16)
    low = (weight - high.astype(F32)).astype(BF16)
    rows = jnp.concatenate([kept_ref[...], core_ref[0], far_ref[0], far_ref[1]], axis=0)
    half = own_ref.shape[1]
    sums = dot_tn(rows, high) + dot_tn(rows, low)
    own_ref[...] = sums[:, :half]
    other_ref[...] = sums[:, half:].astype(BF16)
    for side, d_ref in enumerate((d_own_ref, d_other_ref)):
        span = slice(side * half, (side + 1) * half)
        dots = jnp.dot(rows, d_ref[...], preferred_element_type=F32)
        for choice, mask in enumerate((first, second)):
            route_ref[side, choice : choice + 1, :] = jnp.sum(
                jnp.where(mask[:, span], dots, 0.0), axis=0, keepdims=True
            )


def rows_of(refs):
    parts = []
    for kept_ref, far_ref, core_ref in zip(refs[0::3], refs[1::3], refs[2::3]):
        parts += [kept_ref[...], far_ref[0], core_ref[0], core_ref[1]]
    return jnp.concatenate(parts, axis=0)


def put_rows(refs, value):
    size = refs[0].shape[0]
    for plane in range(len(refs) // 3):
        kept_ref, far_ref, core_ref = refs[3 * plane : 3 * plane + 3]
        part = [value[(4 * plane + n) * size : (4 * plane + n + 1) * size] for n in range(4)]
        kept_ref[...], far_ref[...], core_ref[0], core_ref[1] = part


def experts_kernel(experts, planes, pos_ref, scales_ref, *refs):
    count = 3 * planes
    x_refs, d_refs, refs = refs[:count], refs[count : 2 * count], refs[2 * count :]
    (gate_ref, up_ref, down_ref), out_refs, grad_refs = refs[:3], refs[3 : 3 + count], refs[3 + count :]
    expert = ((pos_ref[0] % 2) * 8 + pos_ref[1]) * experts + pl.program_id(0)
    scale_gate, scale_up, scale_down = [scales_ref[expert, n] for n in range(3)]
    x = rows_of(x_refs)
    gate_value = dot_nt(x, gate_ref[0]) * scale_gate
    up_value = dot_nt(x, up_ref[0]) * scale_up
    grad_activation = dot_nt(rows_of(d_refs), down_ref[0]) * scale_down
    sigmoid_gate, silu_gate = silu_parts(gate_value)
    activation = (silu_gate * up_value).astype(BF16)
    grad_gate = grad_activation * up_value * sigmoid_gate * (1.0 + gate_value * (1.0 - sigmoid_gate))
    grad_gate = grad_gate.astype(BF16)
    grad_up = (grad_activation * silu_gate).astype(BF16)
    part = jnp.dot(activation, down_ref[0], preferred_element_type=F32) * scale_down
    put_rows(out_refs, part.astype(BF16))
    part = jnp.dot(grad_gate, gate_ref[0], preferred_element_type=F32) * scale_gate
    part = part + jnp.dot(grad_up, up_ref[0], preferred_element_type=F32) * scale_up
    put_rows(grad_refs, part.astype(BF16))


SMEM_SPEC = pl.BlockSpec(memory_space=pltpu.SMEM)
PARAMS = pltpu.CompilerParams(vmem_limit_bytes=VMEM_BYTES)


def whole(*shape):
    return pl.BlockSpec(shape, lambda i: (0,) * len(shape))


def after(value, *others):
    return lax.optimization_barrier((value, *others))[0]


def with_core(value):
    return lax.ppermute(value, AXES, [(n, n ^ CORE) for n in range(32)])


def with_near(value):
    return lax.ppermute(value, AXES, [(n, n ^ (ROW if n & CORE else COL)) for n in range(32)])


def with_far(value):
    return lax.ppermute(value, AXES, [(n, n ^ (COL if n & CORE else ROW)) for n in range(32)])


def to_next_plane(value, by):
    return lax.ppermute(value, AXES, [(n, (n + 8 * by) % 32) for n in range(32)])


def per_device_planes(
    tokens, d_output, expert_ids, route_weight, gate_codes, up_codes, down_codes, code_scales
):
    tokens, d_output, ids = tokens.T, d_output.T, expert_ids.T
    gate_codes, up_codes = jnp.swapaxes(gate_codes, 1, 2), jnp.swapaxes(up_codes, 1, 2)
    width, tok_rows = tokens.shape
    experts, hidden = gate_codes.shape[:2]
    expert_count = code_scales.shape[0]
    slots = 2 * tok_rows * ids.shape[0] // expert_count
    message = experts * 2 * slots
    pos = jnp.stack([lax.axis_index("grp"), lax.axis_index("sp")]).astype(jnp.int32)

    earlier = jnp.arange(tok_rows)[:, None] < jnp.arange(tok_rows)[None, :]
    same = (ids[:, None, :, None] == ids[None, :, None, :]) & earlier
    rank = jnp.sum(same.astype(jnp.int32), axis=(0, 2))
    weight = route_weight.T
    high = lax.reduce_precision(weight, 8, 7)
    middle = lax.reduce_precision(weight - high, 8, 7)
    low = weight - high - middle
    info = [ids.astype(F32), rank.astype(F32), high, middle, low]
    info = jnp.concatenate(info + [jnp.zeros((6, tok_rows), F32)], axis=0).astype(BF16)
    tokens = jnp.concatenate([tokens, info], axis=0)
    info_rows = info.shape[0]

    one_type = jax.ShapeDtypeStruct((message, width), BF16)
    two_type = jax.ShapeDtypeStruct((2, message, width), BF16)
    info_spec = pl.BlockSpec((info_rows, tok_rows), lambda i: (width // info_rows, 0))
    block_spec = whole(width, tok_rows)
    one_spec, two_spec = whole(message, width), whole(2, message, width)
    first_spec = pl.BlockSpec((1, message, width), lambda i: (0, 0, 0))
    small_cost = pl.CostEstimate(
        flops=4 * message * 4 * tok_rows * width, bytes_accessed=12 * message * width, transcendentals=0
    )

    def spread(rows, infos, scaled):
        arrived, raw = [], []
        for step in range(4):
            other = with_near(rows)
            raw.append((rows, other))
            kept, core, far = pl.pallas_call(
                functools.partial(pack_kernel, slots, experts, scaled),
                out_shape=[one_type, one_type, two_type],
                grid=(1,),
                in_specs=[SMEM_SPEC] + [info_spec] * 2 + [block_spec] * 2,
                out_specs=[one_spec, one_spec, two_spec],
                compiler_params=PARAMS,
                cost_estimate=small_cost,
                name="pack_gradients" if scaled else "pack_tokens",
            )(pos, *(infos or raw)[step], rows, other)
            far = with_far(far)
            core = with_core(jnp.stack([core, far[1]]))
            arrived += [kept, far, core]
            if step < 3:
                rows = to_next_plane(rows, 1)
        return arrived, raw

    token_rows, infos = spread(tokens, None, False)
    grad_rows, raw_grads = spread(d_output, infos, True)

    expert_rows = 2 * slots
    kept_in = pl.BlockSpec((expert_rows, width), lambda i: (i, 0))
    far_in = pl.BlockSpec((1, expert_rows, width), lambda i: (0, i, 0))
    core_in = pl.BlockSpec((2, expert_rows, width), lambda i: (0, i, 0))
    code_spec = pl.BlockSpec((1, hidden, width), lambda i: (i, 0, 0))

    def run_experts(steps):
        planes = len(steps)
        span = slice(3 * steps[0], 3 * steps[0] + 3 * planes)
        row_count = planes * 4 * expert_rows
        done = pl.pallas_call(
            functools.partial(experts_kernel, experts, planes),
            out_shape=[one_type, one_type, two_type] * (2 * planes),
            grid=(experts,),
            in_specs=[SMEM_SPEC] * 2
            + [kept_in, far_in, core_in] * (2 * planes)
            + [code_spec] * 3,
            out_specs=[kept_in, kept_in, core_in] * (2 * planes),
            compiler_params=PARAMS,
            cost_estimate=pl.CostEstimate(
                flops=experts * row_count * width * hidden * 12,
                bytes_accessed=experts * width * hidden * 6,
                transcendentals=experts * row_count * hidden,
            ),
            name="experts",
        )(pos, code_scales, *token_rows[span], *grad_rows[span], gate_codes, up_codes, down_codes)
        return done[: 3 * planes], done[3 * planes :]

    parts, grads = [], []
    for steps in ((0, 1), (2, 3)):
        more = run_experts(steps)
        parts += more[0]
        grads += more[1]

    own_type = jax.ShapeDtypeStruct((width, tok_rows), F32)
    other_type = jax.ShapeDtypeStruct((width, tok_rows), BF16)
    route_type = jax.ShapeDtypeStruct((2, 2, tok_rows), F32)

    def gather(rows, outputs):
        total, routes, last = None, [None] * 4, []
        for step in (1, 2, 3, 0):
            kept, far, core = rows[3 * step : 3 * step + 3]
            core = with_core(core)
            far = with_far(after(jnp.stack([far, core[1]]), *last))
            last = [far]
            own, other, *route = pl.pallas_call(
                functools.partial(combine_out_kernel if outputs else combine_kernel, slots, experts),
                out_shape=[own_type, other_type] + [route_type] * outputs,
                grid=(1,),
                in_specs=[SMEM_SPEC]
                + [info_spec] * 2
                + [one_spec, first_spec, two_spec]
                + [block_spec] * (2 * outputs),
                out_specs=[block_spec] * 2 + [whole(2, 2, tok_rows)] * outputs,
                compiler_params=PARAMS,
                cost_estimate=small_cost,
                name="sum_outputs" if outputs else "sum_gradients",
            )(pos, *infos[step], kept, core, far, *(raw_grads[step] if outputs else ()))
            routes[step] = route
            other = with_near(other)
            value = own + other.astype(F32)
            if total is not None:
                value = value + to_next_plane(total, 1).astype(F32)
            total = value.astype(BF16)
        return total, routes

    output, routes = gather(parts, 1)
    route = jnp.stack([r[0][0] for r in routes]) + with_near(jnp.stack([r[0][1] for r in routes]))
    d_route = route[0]
    for step in (1, 2, 3):
        d_route = d_route + to_next_plane(route[step], -step)
    d_tokens, _ = gather(grads, 0)
    return (output.T, d_tokens.T, d_route.T)


def solution(mesh):
    planes = mesh.shape["grp"] == 4 and mesh.shape["sp"] == 8
    spec = P(AXES, None)
    codes = P(AXES, None, None)
    return jax.shard_map(
        per_device_planes if planes else per_device,
        mesh=mesh,
        in_specs=(spec, spec, spec, spec, codes, codes, codes, P()),
        out_specs=(spec, spec, spec),
        check_vma=False,
    )
```

```python
import functools

import jax
import jax.numpy as jnp
from jax import lax
from jax.experimental import pallas as pl
from jax.experimental.pallas import tpu as pltpu
from jax.sharding import PartitionSpec as P

AXES = ("grp", "sp")
CORE, COL, ROW = 1, 2, 4
VMEM_BYTES = 56 * 1024 * 1024
F32, BF16 = jnp.float32, jnp.bfloat16


def silu_parts(gate_value):
    sigmoid_gate = 1.0 / (1.0 + jnp.exp(-gate_value))
    return (sigmoid_gate, gate_value * sigmoid_gate)


def per_device(
    tokens, d_output, expert_ids, route_weight, gate_codes, up_codes, down_codes, code_scales
):
    tok_rows, width = tokens.shape
    top_count = expert_ids.shape[1]
    shards_here = gate_codes.shape[0]
    expert_count = code_scales.shape[0]
    group_count = lax.axis_size("grp")
    inner_count = lax.axis_size("sp")
    device_count = group_count * inner_count
    slot_count = 2 * tok_rows * top_count // expert_count
    flat_ids = expert_ids.reshape(-1)
    labels = jnp.arange(expert_count, dtype=jnp.int32)
    onehot = (flat_ids[:, None] == labels[None, :]).astype(jnp.int32)
    slot_rank = jnp.sum((jnp.cumsum(onehot, axis=0) - onehot) * onehot, axis=1)
    target = flat_ids * slot_count + slot_rank
    cells = jnp.arange(expert_count * slot_count, dtype=jnp.int32)
    placing = (target[:, None] == cells[None, :]).astype(jnp.bfloat16)
    token_rows = jnp.repeat(tokens, top_count, axis=0)
    grad_rows = jnp.repeat(d_output, top_count, axis=0).astype(jnp.float32)
    scaled = (route_weight.reshape(-1)[:, None] * grad_rows).astype(jnp.bfloat16)
    payload = jnp.concatenate([token_rows, scaled], axis=1)
    arranged = lax.dot_general(
        placing, payload, (((0,), (0,)), ((), ())), preferred_element_type=jnp.float32
    )
    arranged = arranged.astype(jnp.bfloat16).reshape(expert_count, slot_count, 2 * width)
    arranged = jnp.concatenate([arranged, arranged], axis=0)
    rows_out = arranged[:, :, :width]
    grads_out = arranged[:, :, width:]
    direct_shape = (device_count, shards_here, slot_count, width)
    rows_in, grads_in = (
        lax.all_to_all(rows_out.reshape(direct_shape), AXES, split_axis=0, concat_axis=0, tiled=True),
        lax.all_to_all(grads_out.reshape(direct_shape), AXES, split_axis=0, concat_axis=0, tiled=True),
    )
    device_index = lax.axis_index("grp") * inner_count + lax.axis_index("sp")
    first_shard = device_index * shards_here
    scales_here = lax.dynamic_slice_in_dim(code_scales, first_shard % expert_count, shards_here, 0)
    scale_gate = scales_here[:, 0][None, :, None, None]
    scale_up = scales_here[:, 1][None, :, None, None]
    scale_down = scales_here[:, 2][None, :, None, None]

    def product(spec, left, right):
        return jnp.einsum(spec, left, right, preferred_element_type=jnp.float32)

    gate_value = product("nicd,idh->nich", rows_in, gate_codes) * scale_gate
    up_value = product("nicd,idh->nich", rows_in, up_codes) * scale_up
    sigmoid_gate, silu_gate = silu_parts(gate_value)
    activation = (silu_gate * up_value).astype(jnp.bfloat16)
    expert_part = product("nich,ihd->nicd", activation, down_codes) * scale_down
    grad_activation = product("nicd,ihd->nich", grads_in, down_codes) * scale_down
    grad_gate = (
        grad_activation * up_value * sigmoid_gate * (1.0 + gate_value * (1.0 - sigmoid_gate))
    ).astype(jnp.bfloat16)
    grad_up = (grad_activation * silu_gate).astype(jnp.bfloat16)
    grad_part = product("nich,idh->nicd", grad_gate, gate_codes) * scale_gate
    grad_part = grad_part + product("nich,idh->nicd", grad_up, up_codes) * scale_up
    returned_part, returned_grad = (
        lax.all_to_all(expert_part.astype(BF16), AXES, split_axis=0, concat_axis=0, tiled=True),
        lax.all_to_all(grad_part.astype(BF16), AXES, split_axis=0, concat_axis=0, tiled=True),
    )
    returned_part = returned_part.reshape(2 * expert_count, slot_count, width).astype(F32)
    returned_grad = returned_grad.reshape(2 * expert_count, slot_count, width).astype(F32)
    expert_out = (returned_part[:expert_count] + returned_part[expert_count:]).astype(jnp.bfloat16)
    expert_grad = (returned_grad[:expert_count] + returned_grad[expert_count:]).astype(jnp.bfloat16)
    gathered = jnp.concatenate(
        [expert_out.reshape(-1, width), expert_grad.reshape(-1, width)], axis=1
    )
    picked = jnp.dot(placing, gathered, preferred_element_type=jnp.float32)
    picked_out = picked[:, :width].reshape(tok_rows, top_count, width)
    picked_grad = picked[:, width:].reshape(tok_rows, top_count, width)
    output = jnp.sum(route_weight[:, :, None] * picked_out, axis=1).astype(jnp.bfloat16)
    d_route = jnp.sum(d_output.astype(jnp.float32)[:, None, :] * picked_out, axis=2)
    d_tokens = jnp.sum(picked_grad, axis=1).astype(jnp.bfloat16)
    return (output, d_tokens, d_route)


def hub_onehots(pos_ref, info, slots, experts):
    plane, here = pos_ref[0], pos_ref[1]
    far = jnp.where(here % 2 == 0, ROW, COL)
    tokens = info.shape[1]
    rows = 4 * experts * 2 * slots
    row = lax.broadcasted_iota(jnp.int32, (rows, 1), 0)
    message = row // (2 * slots * experts)
    expert = (row // (2 * slots)) % experts
    side = (row // slots) % 2
    base = (plane % 2) * 8
    device = jnp.where(
        message == 0,
        base + here,
        jnp.where(
            message == 1,
            base + (here ^ CORE),
            jnp.where(message == 2, base + (here ^ far), base + (here ^ far ^ CORE)),
        ),
    )
    cell = ((side * 16 + device) * experts + expert) * slots + row % slots
    column = lax.broadcasted_iota(jnp.int32, (1, tokens), 1)
    partner = (column // (tokens // 2)) * 16 * experts
    first = (partner + info[0:1].astype(jnp.int32)) * slots + info[2:3].astype(jnp.int32)
    second = (partner + info[1:2].astype(jnp.int32)) * slots + info[3:4].astype(jnp.int32)
    weight_first = info[4:5] + info[6:7] + info[8:9]
    weight_second = info[5:6] + info[7:8] + info[9:10]
    return first == cell, second == cell, weight_first, weight_second


def routing(own_ref, other_ref):
    return jnp.concatenate([own_ref[...], other_ref[...]], axis=1).astype(F32)


def dot_nt(left, right):
    return lax.dot_general(left, right, (((1,), (1,)), ((), ())), preferred_element_type=F32)


def dot_tn(left, right):
    return lax.dot_general(left, right, (((0,), (0,)), ((), ())), preferred_element_type=F32)


def pack_kernel(
    slots, experts, scaled, pos_ref, own_info, other_info, own_ref, other_ref, kept_ref, core_ref, far_ref
):
    first, second, weight_first, weight_second = hub_onehots(
        pos_ref, routing(own_info, other_info), slots, experts
    )
    chosen = (first | second).astype(F32).astype(BF16)
    half = own_ref.shape[1]
    rows = dot_nt(chosen[:, :half], own_ref[...]) + dot_nt(chosen[:, half:], other_ref[...])
    if scaled:
        weight = jnp.where(first, weight_first, 0.0) + jnp.where(second, weight_second, 0.0)
        rows = rows * jnp.sum(weight, axis=1, keepdims=True)
    rows = rows.astype(BF16)
    size = rows.shape[0] // 4
    kept_ref[...] = rows[:size]
    core_ref[...] = rows[size : 2 * size]
    far_ref[0] = rows[2 * size : 3 * size]
    far_ref[1] = rows[3 * size :]


def combine_kernel(
    slots, experts, pos_ref, own_info, other_info, kept_ref, core_ref, far_ref, own_ref, other_ref
):
    first, second, _, _ = hub_onehots(pos_ref, routing(own_info, other_info), slots, experts)
    chosen = (first | second).astype(F32).astype(BF16)
    rows = jnp.concatenate([kept_ref[...], core_ref[0], far_ref[0], far_ref[1]], axis=0)
    half = own_ref.shape[1]
    sums = dot_tn(rows, chosen)
    own_ref[...] = sums[:, :half]
    other_ref[...] = sums[:, half:].astype(BF16)


def combine_out_kernel(
    slots,
    experts,
    pos_ref,
    own_info,
    other_info,
    kept_ref,
    core_ref,
    far_ref,
    d_own_ref,
    d_other_ref,
    own_ref,
    other_ref,
    route_ref,
):
    first, second, weight_first, weight_second = hub_onehots(
        pos_ref, routing(own_info, other_info), slots, experts
    )
    weight = jnp.where(first, weight_first, 0.0) + jnp.where(second, weight_second, 0.0)
    high = weight.astype(BF16)
    low = (weight - high.astype(F32)).astype(BF16)
    rows = jnp.concatenate([kept_ref[...], core_ref[0], far_ref[0], far_ref[1]], axis=0)
    half = own_ref.shape[1]
    sums = dot_tn(rows, high) + dot_tn(rows, low)
    own_ref[...] = sums[:, :half]
    other_ref[...] = sums[:, half:].astype(BF16)
    for side, d_ref in enumerate((d_own_ref, d_other_ref)):
        span = slice(side * half, (side + 1) * half)
        dots = jnp.dot(rows, d_ref[...], preferred_element_type=F32)
        for choice, mask in enumerate((first, second)):
            route_ref[side, choice : choice + 1, :] = jnp.sum(
                jnp.where(mask[:, span], dots, 0.0), axis=0, keepdims=True
            )


def rows_of(refs):
    parts = []
    for kept_ref, far_ref, core_ref in zip(refs[0::3], refs[1::3], refs[2::3]):
        parts += [kept_ref[...], far_ref[0], core_ref[0], core_ref[1]]
    return jnp.concatenate(parts, axis=0)


def put_rows(refs, value):
    size = refs[0].shape[0]
    for plane in range(len(refs) // 3):
        kept_ref, far_ref, core_ref = refs[3 * plane : 3 * plane + 3]
        part = [value[(4 * plane + n) * size : (4 * plane + n + 1) * size] for n in range(4)]
        kept_ref[...], far_ref[...], core_ref[0], core_ref[1] = part


def experts_kernel(experts, planes, pos_ref, scales_ref, *refs):
    count = 3 * planes
    x_refs, d_refs, refs = refs[:count], refs[count : 2 * count], refs[2 * count :]
    (gate_ref, up_ref, down_ref), out_refs, grad_refs = refs[:3], refs[3 : 3 + count], refs[3 + count :]
    expert = ((pos_ref[0] % 2) * 8 + pos_ref[1]) * experts + pl.program_id(0)
    scale_gate, scale_up, scale_down = [scales_ref[expert, n] for n in range(3)]
    x = rows_of(x_refs)
    gate_value = dot_nt(x, gate_ref[0]) * scale_gate
    up_value = dot_nt(x, up_ref[0]) * scale_up
    grad_activation = dot_nt(rows_of(d_refs), down_ref[0]) * scale_down
    sigmoid_gate, silu_gate = silu_parts(gate_value)
    activation = (silu_gate * up_value).astype(BF16)
    grad_gate = grad_activation * up_value * sigmoid_gate * (1.0 + gate_value * (1.0 - sigmoid_gate))
    grad_gate = grad_gate.astype(BF16)
    grad_up = (grad_activation * silu_gate).astype(BF16)
    part = jnp.dot(activation, down_ref[0], preferred_element_type=F32) * scale_down
    put_rows(out_refs, part.astype(BF16))
    part = jnp.dot(grad_gate, gate_ref[0], preferred_element_type=F32) * scale_gate
    part = part + jnp.dot(grad_up, up_ref[0], preferred_element_type=F32) * scale_up
    put_rows(grad_refs, part.astype(BF16))


SMEM_SPEC = pl.BlockSpec(memory_space=pltpu.SMEM)
PARAMS = pltpu.CompilerParams(vmem_limit_bytes=VMEM_BYTES)


def whole(*shape):
    return pl.BlockSpec(shape, lambda i: (0,) * len(shape))


def after(value, *others):
    return lax.optimization_barrier((value, *others))[0]


def with_core(value):
    return lax.ppermute(value, AXES, [(n, n ^ CORE) for n in range(32)])


def with_near(value):
    return lax.ppermute(value, AXES, [(n, n ^ (ROW if n & CORE else COL)) for n in range(32)])


def with_far(value):
    return lax.ppermute(value, AXES, [(n, n ^ (COL if n & CORE else ROW)) for n in range(32)])


def to_next_plane(value, by):
    return lax.ppermute(value, AXES, [(n, (n + 8 * by) % 32) for n in range(32)])


def per_device_planes(
    tokens, d_output, expert_ids, route_weight, gate_codes, up_codes, down_codes, code_scales
):
    tokens, d_output, ids = tokens.T, d_output.T, expert_ids.T
    gate_codes, up_codes = jnp.swapaxes(gate_codes, 1, 2), jnp.swapaxes(up_codes, 1, 2)
    width, tok_rows = tokens.shape
    experts, hidden = gate_codes.shape[:2]
    expert_count = code_scales.shape[0]
    slots = 2 * tok_rows * ids.shape[0] // expert_count
    message = experts * 2 * slots
    pos = jnp.stack([lax.axis_index("grp"), lax.axis_index("sp")]).astype(jnp.int32)

    earlier = jnp.arange(tok_rows)[:, None] < jnp.arange(tok_rows)[None, :]
    same = (ids[:, None, :, None] == ids[None, :, None, :]) & earlier
    rank = jnp.sum(same.astype(jnp.int32), axis=(0, 2))
    weight = route_weight.T
    high = lax.reduce_precision(weight, 8, 7)
    middle = lax.reduce_precision(weight - high, 8, 7)
    low = weight - high - middle
    info = [ids.astype(F32), rank.astype(F32), high, middle, low]
    info = jnp.concatenate(info + [jnp.zeros((6, tok_rows), F32)], axis=0).astype(BF16)
    tokens = jnp.concatenate([tokens, info], axis=0)
    info_rows = info.shape[0]

    one_type = jax.ShapeDtypeStruct((message, width), BF16)
    two_type = jax.ShapeDtypeStruct((2, message, width), BF16)
    info_spec = pl.BlockSpec((info_rows, tok_rows), lambda i: (width // info_rows, 0))
    block_spec = whole(width, tok_rows)
    one_spec, two_spec = whole(message, width), whole(2, message, width)
    first_spec = pl.BlockSpec((1, message, width), lambda i: (0, 0, 0))
    small_cost = pl.CostEstimate(
        flops=4 * message * 4 * tok_rows * width, bytes_accessed=12 * message * width, transcendentals=0
    )

    def spread(rows, infos, scaled):
        arrived, raw = [], []
        for step in range(4):
            other = with_near(rows)
            raw.append((rows, other))
            kept, core, far = pl.pallas_call(
                functools.partial(pack_kernel, slots, experts, scaled),
                out_shape=[one_type, one_type, two_type],
                grid=(1,),
                in_specs=[SMEM_SPEC] + [info_spec] * 2 + [block_spec] * 2,
                out_specs=[one_spec, one_spec, two_spec],
                compiler_params=PARAMS,
                cost_estimate=small_cost,
                name="pack_gradients" if scaled else "pack_tokens",
            )(pos, *(infos or raw)[step], rows, other)
            far = with_far(far)
            core = with_core(jnp.stack([core, far[1]]))
            arrived += [kept, far, core]
            if step < 3:
                rows = to_next_plane(rows, 1)
        return arrived, raw

    token_rows, infos = spread(tokens, None, False)
    grad_rows, raw_grads = spread(d_output, infos, True)

    expert_rows = 2 * slots
    kept_in = pl.BlockSpec((expert_rows, width), lambda i: (i, 0))
    far_in = pl.BlockSpec((1, expert_rows, width), lambda i: (0, i, 0))
    core_in = pl.BlockSpec((2, expert_rows, width), lambda i: (0, i, 0))
    code_spec = pl.BlockSpec((1, hidden, width), lambda i: (i, 0, 0))

    def run_experts(steps):
        planes = len(steps)
        span = slice(3 * steps[0], 3 * steps[0] + 3 * planes)
        row_count = planes * 4 * expert_rows
        done = pl.pallas_call(
            functools.partial(experts_kernel, experts, planes),
            out_shape=[one_type, one_type, two_type] * (2 * planes),
            grid=(experts,),
            in_specs=[SMEM_SPEC] * 2
            + [kept_in, far_in, core_in] * (2 * planes)
            + [code_spec] * 3,
            out_specs=[kept_in, kept_in, core_in] * (2 * planes),
            compiler_params=PARAMS,
            cost_estimate=pl.CostEstimate(
                flops=experts * row_count * width * hidden * 12,
                bytes_accessed=experts * width * hidden * 6,
                transcendentals=experts * row_count * hidden,
            ),
            name="experts",
        )(pos, code_scales, *token_rows[span], *grad_rows[span], gate_codes, up_codes, down_codes)
        return done[: 3 * planes], done[3 * planes :]

    parts, grads = [], []
    for steps in ((0, 1), (2, 3)):
        more = run_experts(steps)
        parts += more[0]
        grads += more[1]

    own_type = jax.ShapeDtypeStruct((width, tok_rows), F32)
    other_type = jax.ShapeDtypeStruct((width, tok_rows), BF16)
    route_type = jax.ShapeDtypeStruct((2, 2, tok_rows), F32)

    def gather(rows, outputs):
        total, routes, last = None, [None] * 4, []
        for step in (1, 2, 3, 0):
            kept, far, core = rows[3 * step : 3 * step + 3]
            core = with_core(core)
            far = with_far(after(jnp.stack([far, core[1]]), *last))
            last = [far]
            own, other, *route = pl.pallas_call(
                functools.partial(combine_out_kernel if outputs else combine_kernel, slots, experts),
                out_shape=[own_type, other_type] + [route_type] * outputs,
                grid=(1,),
                in_specs=[SMEM_SPEC]
                + [info_spec] * 2
                + [one_spec, first_spec, two_spec]
                + [block_spec] * (2 * outputs),
                out_specs=[block_spec] * 2 + [whole(2, 2, tok_rows)] * outputs,
                compiler_params=PARAMS,
                cost_estimate=small_cost,
                name="sum_outputs" if outputs else "sum_gradients",
            )(pos, *infos[step], kept, core, far, *(raw_grads[step] if outputs else ()))
            routes[step] = route
            other = with_near(other)
            value = own + other.astype(F32)
            if total is not None:
                value = value + to_next_plane(total, 1).astype(F32)
            total = value.astype(BF16)
        return total, routes

    d_tokens, _ = gather(grads, 0)
    output, routes = gather(parts, 1)
    route = jnp.stack([r[0][0] for r in routes]) + with_near(jnp.stack([r[0][1] for r in routes]))
    d_route = route[0]
    for step in (1, 2, 3):
        d_route = d_route + to_next_plane(route[step], -step)
    return (output.T, d_tokens.T, d_route.T)


def solution(mesh):
    planes = mesh.shape["grp"] == 4 and mesh.shape["sp"] == 8
    spec = P(AXES, None)
    codes = P(AXES, None, None)
    return jax.shard_map(
        per_device_planes if planes else per_device,
        mesh=mesh,
        in_specs=(spec, spec, spec, spec, codes, codes, codes, P()),
        out_specs=(spec, spec, spec),
        check_vma=False,
    )
```
